256 devices in a mesh: ctx: 32 (over y, x, z_lo), head: 8 (over z_hi, core).
Axes of the slice: x: 4, y: 4, z: 8 (z_hi: 4, z_lo: 2; z = z_hi * 2 + z_lo), core: 2. Of those that a mesh axis runs over, the one named last changes fastest.
Arguments:
- query: bfloat16 [8192, 16384], P('ctx', 'head'), may hold values from -42.5 to 42.5
- keys: bfloat16 [8192, 1024], P(('ctx', 'head')), may hold values from -6 to 6
- values: bfloat16 [8192, 1024], P(('ctx', 'head')), may hold values from -6 to 6
- d_out: bfloat16 [8192, 16384], P('ctx', 'head'), may hold values from -6 to 6
- lengths: int32 [16], replicated, may hold values from 1 to 8, as said below
Outputs:
- attn_out: bfloat16 [8192, 16384], P('ctx', 'head')
- d_query: bfloat16 [8192, 16384], P('ctx', 'head')
- d_keys: bfloat16 [8192, 1024], P(('ctx', 'head'))
- d_values: bfloat16 [8192, 1024], P(('ctx', 'head'))
The draws below stay inside these ranges and needn't reach their ends.
Inputs may be any that keep to these rules, and one draw needn't show every extreme that they name: `lengths`: the documents lie in order from token 0 and together cover all 8192 tokens; one document has exactly 1024 tokens.
All inputs are finite; a program needn't handle non-finite values.
Results may differ from the reference program's by a relative error of at most 0.04.
Values may be sent and summed in bfloat16 or wider, within the bound.
A program may use at most 64 MiB of HBM per device.

```python
import math
import jax
import jax.numpy as jnp
from jax import lax

QH = 128
KVH = 8
DH = 128
TOK_DEV = 256
BLK = 128
DOC_DEVS = 4
DOC_MOST = 1024
TOKENS = 8192
DOCS = 16
N_CTX = 32


def pair_draw(key):
    key_base = jnp.clip(jax.random.normal(jax.random.fold_in(key, 101), (TOKENS, KVH, DH), jnp.float32), -6.0, 6.0)
    query_base = jnp.clip(jax.random.normal(jax.random.fold_in(key, 102), (TOKENS, QH, DH), jnp.float32), -6.0, 6.0)
    return (query_base.reshape(TOKENS, QH * DH), key_base.reshape(TOKENS, KVH * DH))


def draw_query(key, part):
    return pair_draw(key)[0].astype(jnp.bfloat16)


def draw_keys(key, part):
    return pair_draw(key)[1].astype(jnp.bfloat16)


def draw_lengths(key, part):
    key = jax.random.fold_in(key, 7)
    most_units = DOC_MOST // BLK
    others = DOCS - 1
    spare = TOKENS // BLK - most_units - others
    doc_index = jnp.arange(others, dtype=jnp.int32)

    def place_unit(step, current):
        scores = jax.random.randint(jax.random.fold_in(key, 1000 + step), (others,), 0, 1 << 20).astype(jnp.int32)
        scores = scores * others + doc_index
        scores = jnp.where(current < most_units, scores, -1)
        chosen = jnp.argmax(scores).astype(jnp.int32)
        return current + (doc_index == chosen).astype(jnp.int32)
    filled = lax.fori_loop(0, spare, place_unit, jnp.ones((others,), jnp.int32))
    where_most = jax.random.randint(jax.random.fold_in(key, 5), (), 0, DOCS).astype(jnp.int32)
    slots = jnp.arange(DOCS, dtype=jnp.int32)
    before = filled[jnp.clip(slots, 0, others - 1)]
    after = filled[jnp.clip(slots - 1, 0, others - 1)]
    return jnp.where(slots < where_most, before, jnp.where(slots == where_most, most_units, after)).astype(jnp.int32)


def level_of(key, extent, split, least, largest):
    gain, own = 1.0, jax.random.fold_in(key, 6)
    for axis_at, blocks in split:
        heights = jnp.exp(jax.random.uniform(jax.random.fold_in(own, axis_at), (blocks,), jnp.float32, least / len(split), largest / len(split)))
        gain = gain * jnp.repeat(heights, extent[axis_at] // blocks).reshape([-1 if axis == axis_at else 1 for axis in range(len(extent))])
    return gain


def bell_draw(own_key, shape, deviation, bound, split=(), held_as=jnp.bfloat16):
    factor_of = level_of(own_key, shape, split, -0.22, 0.18) if split else 1.0
    array = jax.random.normal(own_key, shape, jnp.float32) * deviation * factor_of
    return jnp.minimum(jnp.maximum(array, -bound), bound).astype(held_as)


def setup_inputs(seed: int = 0) -> dict:
    arg_keys = jax.random.split(jax.random.key(seed), 6)
    query = draw_query(jax.random.fold_in(arg_keys[5], 71), 0)
    keys = draw_keys(jax.random.fold_in(arg_keys[5], 71), 0)
    values = bell_draw(arg_keys[2], (TOKENS, KVH * DH), 1.0, 6.0, ((0, 256),))
    d_out = bell_draw(arg_keys[3], (TOKENS, QH * DH), 1.0, 6.0, ((0, 32), (1, 8)))
    lengths = draw_lengths(jax.random.fold_in(arg_keys[5], 71), 0)
    return dict(query=query, keys=keys, values=values, d_out=d_out, lengths=lengths)


masked_score = -1e+30

def document_ids(positions, doc_ends):
    return lax.optimization_barrier(jnp.sum((positions[:, None] >= doc_ends[None, :]).astype(jnp.int32), axis=1)).astype(jnp.int32)

def reference(query, keys, values, d_out, lengths):
    group_size = QH // KVH
    score_scale = 1.0 / math.sqrt(DH)
    doc_ends = (jnp.cumsum(lengths).astype(jnp.int32) * BLK).astype(jnp.int32)
    positions = jnp.arange(TOKENS, dtype=jnp.int32)
    doc_ids = document_ids(positions, doc_ends)
    margin = DOC_DEVS * TOK_DEV
    window = margin + TOK_DEV
    keys_padded = jnp.concatenate([jnp.zeros((margin, KVH * DH), keys.dtype), keys], axis=0)
    values_padded = jnp.concatenate([jnp.zeros((margin, KVH * DH), values.dtype), values], axis=0)
    doc_padded = jnp.concatenate([-jnp.ones((margin,), jnp.int32), doc_ids], axis=0)
    pos_padded = jnp.concatenate([jnp.arange(margin, dtype=jnp.int32) - margin, positions], axis=0)

    def block_step(running, block_index):
        keys_acc, values_acc = running
        row_start = (block_index * TOK_DEV).astype(jnp.int32)
        query_rows = lax.dynamic_slice_in_dim(query, row_start, TOK_DEV, 0).reshape(TOK_DEV, KVH, group_size, DH).astype(jnp.float32)
        dout_rows = lax.dynamic_slice_in_dim(d_out, row_start, TOK_DEV, 0).reshape(TOK_DEV, KVH, group_size, DH).astype(jnp.float32)
        key_rows = lax.dynamic_slice_in_dim(keys_padded, row_start, window, 0).reshape(window, KVH, DH).astype(jnp.float32)
        value_rows = lax.dynamic_slice_in_dim(values_padded, row_start, window, 0).reshape(window, KVH, DH).astype(jnp.float32)
        query_doc = lax.dynamic_slice_in_dim(doc_ids, row_start, TOK_DEV, 0)
        query_pos = lax.dynamic_slice_in_dim(positions, row_start, TOK_DEV, 0)
        key_doc = lax.dynamic_slice_in_dim(doc_padded, row_start, window, 0)
        key_pos = lax.dynamic_slice_in_dim(pos_padded, row_start, window, 0)
        allowed = (query_doc[:, None] == key_doc[None, :]) & (key_pos[None, :] <= query_pos[:, None])
        scores = jnp.einsum('tkgd,skd->kgts', query_rows, key_rows) * score_scale
        scores = jnp.where(allowed[None, None], scores, masked_score)
        row_max = lax.optimization_barrier(jnp.max(scores, axis=-1))
        log_norm = row_max + jnp.log(lax.optimization_barrier(jnp.sum(jnp.exp(scores - row_max[..., None]), axis=-1)))
        weights = jnp.exp(scores - log_norm[..., None])
        weights_low = weights.astype(jnp.bfloat16)
        output = jnp.einsum('kgts,skd->tkgd', weights_low.astype(jnp.float32), value_rows).astype(jnp.bfloat16)
        row_delta = lax.optimization_barrier(jnp.sum(dout_rows * output.astype(jnp.float32), axis=-1)).transpose(1, 2, 0)
        grad_probs = jnp.einsum('tkgd,skd->kgts', dout_rows, value_rows)
        grad_scores = (weights * (grad_probs - row_delta[..., None])).astype(jnp.bfloat16)
        grad_query = (jnp.einsum('kgts,skd->tkgd', grad_scores.astype(jnp.float32), key_rows) * score_scale).astype(jnp.bfloat16)
        grad_keys = jnp.einsum('kgts,tkgd->skd', grad_scores.astype(jnp.float32), query_rows) * score_scale
        grad_values = jnp.einsum('kgts,tkgd->skd', weights_low.astype(jnp.float32), dout_rows)
        keys_acc = lax.dynamic_update_slice_in_dim(keys_acc, lax.dynamic_slice_in_dim(keys_acc, row_start, window, 0) + grad_keys.reshape(window, KVH * DH), row_start, 0)
        values_acc = lax.dynamic_update_slice_in_dim(values_acc, lax.dynamic_slice_in_dim(values_acc, row_start, window, 0) + grad_values.reshape(window, KVH * DH), row_start, 0)
        return ((keys_acc, values_acc), (output.reshape(TOK_DEV, QH * DH), grad_query.reshape(TOK_DEV, QH * DH)))
    initial = (jnp.zeros((margin + TOKENS, KVH * DH), jnp.float32), jnp.zeros((margin + TOKENS, KVH * DH), jnp.float32))
    (keys_acc, values_acc), (outputs, query_grads) = lax.scan(block_step, initial, jnp.arange(N_CTX, dtype=jnp.int32))
    attn_out = outputs.reshape(TOKENS, QH * DH)
    d_query = query_grads.reshape(TOKENS, QH * DH)
    return (attn_out, d_query, keys_acc[margin:].astype(jnp.bfloat16), values_acc[margin:].astype(jnp.bfloat16))
```

```python
import functools
import math

import jax
import jax.numpy as jnp
from jax import lax
from jax.experimental import pallas as pl
from jax.experimental.pallas import tpu as pltpu
from jax.sharding import PartitionSpec as P

QH = 128
KVH = 8
DH = 128
BLK = 128
GROUP = QH // KVH
PAIRS = GROUP // 2
MESH = pl.DeviceIdType.MESH
BF = jnp.bfloat16
F32 = jnp.float32
SCALE = 1.0 / math.sqrt(DH)
C2 = SCALE * math.log2(math.e)
MASKED = -1e30


def dot(a, b):
    return lax.dot_general(a, b, (((1,), (0,)), ((), ())), preferred_element_type=F32)


def kernel(
    n_ctx, n_head,
    len_ref, q_hbm, k_hbm, v_hbm, do_hbm,
    o_hbm, dq_hbm, dk_ref, dv_ref,
    q_ref, do_ref, k_ref, v_ref, qt, dot_t, kv, kk, vv, kt, vte, tri,
    m_run, m_tile, acc, p_all, dp_all, dqt, dk_acc, dv_acc,
    o_out, dq_out, gsend, grecv, gown, gfin, stage,
    load_sem, out_sem, a_send, a_recv, c_send, c_recv, g_send, g_recv, b_send, b_recv,
):
    c = lax.axis_index("ctx")
    h = lax.axis_index("head")

    def peer(j):
        return (c, lax.rem(h + j, n_head))

    def after(o):
        return (lax.rem(c + o, n_ctx), h)

    def before(o):
        return (lax.rem(c + n_ctx - o, n_ctx), h)

    loads = [
        pltpu.make_async_copy(k_hbm, k_ref, load_sem.at[0]),
        pltpu.make_async_copy(v_hbm, v_ref, load_sem.at[1]),
        pltpu.make_async_copy(q_hbm, q_ref, load_sem.at[2]),
        pltpu.make_async_copy(do_hbm, do_ref, load_sem.at[3]),
    ]
    for copy in loads:
        copy.start()

    barrier = pltpu.get_barrier_semaphore()
    for j in range(1, n_head):
        pl.semaphore_signal(barrier, inc=1, device_id=peer(j), device_id_type=MESH)
    for o in range(1, 5):
        pl.semaphore_signal(barrier, inc=1, device_id=after(o), device_id_type=MESH)
        pl.semaphore_signal(barrier, inc=1, device_id=before(o), device_id_type=MESH)

    loads[0].wait()
    loads[1].wait()
    for j in range(n_head):
        stage[j, 0] = k_ref[:, j * DH:(j + 1) * DH]
        stage[j, 1] = v_ref[:, j * DH:(j + 1) * DH]
    kv[0, h] = stage[h]
    pl.semaphore_wait(barrier, n_head - 1 + 8)

    heads_in = []
    for j in range(1, n_head):
        copy = pltpu.make_async_remote_copy(
            src_ref=stage.at[lax.rem(h + j, n_head)], dst_ref=kv.at[0, h],
            send_sem=a_send.at[j - 1], recv_sem=a_recv.at[j - 1],
            device_id=peer(j), device_id_type=MESH)
        copy.start()
        heads_in.append(copy)

    loads[2].wait()
    loads[3].wait()

    def transpose_pair(i, carry):
        u = i // PAIRS
        g = lax.rem(i, PAIRS)
        rows = pl.ds(pl.multiple_of(u * BLK, BLK), BLK)
        for e in range(2):
            cols = pl.ds(pl.multiple_of((2 * g + e) * DH, DH), DH)
            qt[i, :, e * BLK:(e + 1) * BLK] = q_ref[rows, cols].T
            dot_t[i, :, e * BLK:(e + 1) * BLK] = do_ref[rows, cols].T
        m_run[i] = jnp.full((1, 2 * BLK), 2 * MASKED, F32)
        acc[i] = jnp.zeros((DH + 16, 2 * BLK), F32)
        dqt[i] = jnp.zeros((DH, 2 * BLK), F32)
        return carry

    lax.fori_loop(0, 2 * PAIRS, transpose_pair, 0)
    key_at = lax.broadcasted_iota(jnp.int32, (BLK, 2 * BLK), 0)
    query_at = lax.rem(lax.broadcasted_iota(jnp.int32, (BLK, 2 * BLK), 1), BLK)
    tri[...] = jnp.where(key_at > query_at, MASKED, 0.0)
    dk_acc[...] = jnp.zeros_like(dk_acc)
    dv_acc[...] = jnp.zeros_like(dv_acc)

    starts = []
    for u in range(2):
        end = jnp.int32(0)
        first = jnp.int32(0)
        for d in range(16):
            end = end + len_ref[d]
            first = jnp.where(end <= 2 * c + u, end, first)
        starts.append(first)

    for copy in heads_in:
        copy.wait()

    ctx_in = []
    for o in range(1, 5):
        part = kv.at[0] if o < 4 else kv.at[0, pl.ds(n_head // 2, n_head // 2)]
        there = kv.at[o] if o < 4 else kv.at[4, pl.ds(n_head // 2, n_head // 2)]
        copy = pltpu.make_async_remote_copy(
            src_ref=part, dst_ref=there,
            send_sem=c_send.at[o - 1], recv_sem=c_recv.at[o - 1],
            device_id=after(o), device_id_type=MESH)
        copy.start()
        ctx_in.append(copy)

    def prepare(t):
        if t < 4:
            key = kv[t, :, 0].reshape(2 * BLK, DH)
            val = kv[t, :, 1].reshape(2 * BLK, DH)
        else:
            half = n_head // 2
            key = jnp.concatenate((kv[4, half:, 0].reshape(BLK, DH), kv[0, :half, 0].reshape(BLK, DH)), 0)
            val = jnp.concatenate((kv[4, half:, 1].reshape(BLK, DH), kv[0, :half, 1].reshape(BLK, DH)), 0)
        kk[t] = key
        vv[t] = val
        kt[t] = key.T
        vte[t, :DH] = val.T
        vte[t, DH:] = jnp.ones((16, 2 * BLK), BF)

    def place(u, t):
        return t if u == 1 else t - 1

    def forward(u, t):
        first_unit = 2 * c - 2 * t if t < 4 else 2 * c - 7
        bias0 = jnp.where(first_unit >= starts[u], 0.0, MASKED).astype(F32)
        bias1 = jnp.where(first_unit + 1 >= starts[u], 0.0, MASKED).astype(F32)
        slot = place(u, t)

        def one(g):
            i = u * PAIRS + g
            scores = dot(kk[t], qt[i])
            dp_all[slot, i] = dot(vv[t], dot_t[i])
            low = scores[:BLK] + bias0
            high = scores[BLK:] + (tri[...] if t in (0, 4) else bias1)
            old = m_run[i]
            new = jnp.maximum(old, jnp.max(jnp.maximum(low, high), axis=0, keepdims=True))
            p_low = jnp.exp2((low - new) * C2).astype(BF)
            p_high = jnp.exp2((high - new) * C2).astype(BF)
            weights = jnp.concatenate((p_low, p_high), 0)
            p_all[slot, i] = weights
            m_tile[slot, i] = new
            m_run[i] = new
            acc[i] = acc[i] * jnp.exp2((old - new) * C2) + dot(vte[t], weights)

        def body(step, carry):
            one(2 * step)
            one(2 * step + 1)
            return carry

        lax.fori_loop(0, PAIRS // 2, body, 0)

    prepare(0)
    forward(1, 0)
    for o in range(1, 4):
        ctx_in[o - 1].wait_recv()
        prepare(o)
        forward(0, o)
        forward(1, o)
    ctx_in[3].wait_recv()
    prepare(4)
    forward(0, 4)

    def finish(i, carry):
        u = i // PAIRS
        g = lax.rem(i, PAIRS)
        rows = pl.ds(pl.multiple_of(u * BLK, BLK), BLK)
        total = acc[i, DH:DH + 1]
        inverse = 1.0 / total
        low = (acc[i, :DH] * inverse).astype(BF)
        delta = jnp.sum(low.astype(F32) * dot_t[i].astype(F32), axis=0, keepdims=True)
        acc[i, DH:DH + 1] = inverse
        acc[i, DH + 8:DH + 9] = delta
        for e in range(2):
            cols = pl.ds(pl.multiple_of((2 * g + e) * DH, DH), DH)
            o_out[rows, cols] = low[:, e * BLK:(e + 1) * BLK].T
        return carry

    lax.fori_loop(0, 2 * PAIRS, finish, 0)
    o_copy = pltpu.make_async_copy(o_out, o_hbm, out_sem.at[0])
    o_copy.start()

    def backward(u, t):
        slot = place(u, t)

        def one(g):
            i = u * PAIRS + g
            rows = pl.ds(u * BLK, BLK)
            first = pl.ds(pl.multiple_of(2 * g * DH, DH), DH)
            second = pl.ds(pl.multiple_of((2 * g + 1) * DH, DH), DH)
            queries = jnp.concatenate((q_ref[rows, first], q_ref[rows, second]), 0)
            cotangents = jnp.concatenate((do_ref[rows, first], do_ref[rows, second]), 0)
            factor = jnp.exp2((m_tile[slot, i] - m_run[i]) * C2) * acc[i, DH:DH + 1]
            weights = p_all[slot, i].astype(F32) * factor
            ds = (weights * (dp_all[slot, i] - acc[i, DH + 8:DH + 9])).astype(BF)
            dqt[i] += dot(kt[t], ds)
            return dot(ds, queries), dot(weights.astype(BF), cotangents)

        def body(step, carry):
            dk0, dv0 = one(2 * step)
            dk1, dv1 = one(2 * step + 1)
            dk_acc[t] += dk0 + dk1
            dv_acc[t] += dv0 + dv1
            return carry

        lax.fori_loop(0, PAIRS // 2, body, 0)

    half = n_head // 2
    grads_out = []

    def send(o):
        if o < 4:
            gsend[o, :, 0] = (dk_acc[o] * SCALE).astype(BF).reshape(n_head, 32, DH)
            gsend[o, :, 1] = dv_acc[o].astype(BF).reshape(n_head, 32, DH)
            part, there = gsend.at[o], grecv.at[o]
        else:
            gsend[4, half:, 0] = (dk_acc[4, :BLK] * SCALE).astype(BF).reshape(half, 32, DH)
            gsend[4, half:, 1] = dv_acc[4, :BLK].astype(BF).reshape(half, 32, DH)
            part, there = gsend.at[4, pl.ds(half, half)], grecv.at[4, pl.ds(half, half)]
        copy = pltpu.make_async_remote_copy(
            src_ref=part, dst_ref=there,
            send_sem=g_send.at[o - 1], recv_sem=g_recv.at[o - 1],
            device_id=before(o), device_id_type=MESH)
        copy.start()
        grads_out.append(copy)

    backward(0, 4)
    send(4)
    for o in range(3, 0, -1):
        backward(0, o)
        backward(1, o)
        send(o)
    backward(1, 0)

    def finish_query(i, carry):
        u = i // PAIRS
        g = lax.rem(i, PAIRS)
        rows = pl.ds(pl.multiple_of(u * BLK, BLK), BLK)
        low = (dqt[i] * SCALE).astype(BF)
        for e in range(2):
            cols = pl.ds(pl.multiple_of((2 * g + e) * DH, DH), DH)
            dq_out[rows, cols] = low[:, e * BLK:(e + 1) * BLK].T
        return carry

    lax.fori_loop(0, 2 * PAIRS, finish_query, 0)
    dq_copy = pltpu.make_async_copy(dq_out, dq_hbm, out_sem.at[1])
    dq_copy.start()

    for copy in grads_out:
        copy.wait_recv()
    dk_low = dk_acc[0, :BLK] + dk_acc[4, BLK:]
    dv_low = dv_acc[0, :BLK] + dv_acc[4, BLK:]
    for n, (low, high, scale) in enumerate(
        ((dk_low, dk_acc[0, BLK:], SCALE), (dv_low, dv_acc[0, BLK:], 1.0))):
        low = (low * scale).reshape(half, 32, DH)
        high = (high * scale).reshape(half, 32, DH)
        for o in range(1, 4):
            low = low + grecv[o, :half, n].astype(F32)
            high = high + grecv[o, half:, n].astype(F32)
        high = high + grecv[4, half:, n].astype(F32)
        gown[:half, n] = low.astype(BF)
        gown[half:, n] = high.astype(BF)

    gfin[h] = gown[h]
    heads_out = []
    for j in range(1, n_head):
        copy = pltpu.make_async_remote_copy(
            src_ref=gown.at[lax.rem(h + j, n_head)], dst_ref=gfin.at[h],
            send_sem=b_send.at[j - 1], recv_sem=b_recv.at[j - 1],
            device_id=peer(j), device_id_type=MESH)
        copy.start()
        heads_out.append(copy)
    for copy in ctx_in:
        copy.wait_send()
    for copy in grads_out:
        copy.wait_send()
    for copy in heads_out:
        copy.wait()
    for j in range(n_head):
        dk_ref[:, j * DH:(j + 1) * DH] = gfin[j, 0]
        dv_ref[:, j * DH:(j + 1) * DH] = gfin[j, 1]
    o_copy.wait()
    dq_copy.wait()


def local(query, keys, values, d_out, lengths):
    n_ctx = lax.axis_size("ctx")
    n_head = lax.axis_size("head")
    pairs = 2 * PAIRS
    hbm = pl.BlockSpec(memory_space=pl.ANY)
    vmem = pl.BlockSpec(memory_space=pltpu.VMEM)
    wide = (2 * BLK, GROUP * DH)
    dma = pltpu.SemaphoreType.DMA
    return pl.pallas_call(
        functools.partial(kernel, n_ctx, n_head),
        name="attention",
        out_shape=(
            jax.ShapeDtypeStruct(query.shape, BF),
            jax.ShapeDtypeStruct(query.shape, BF),
            jax.ShapeDtypeStruct(keys.shape, BF),
            jax.ShapeDtypeStruct(keys.shape, BF),
        ),
        in_specs=[pl.BlockSpec(memory_space=pltpu.SMEM), hbm, hbm, hbm, hbm],
        out_specs=(hbm, hbm, vmem, vmem),
        scratch_shapes=[
            pltpu.VMEM(wide, BF),
            pltpu.VMEM(wide, BF),
            pltpu.VMEM(keys.shape, BF),
            pltpu.VMEM(keys.shape, BF),
            pltpu.VMEM((pairs, DH, 2 * BLK), BF),
            pltpu.VMEM((pairs, DH, 2 * BLK), BF),
            pltpu.VMEM((5, n_head, 2, 32, DH), BF),
            pltpu.VMEM((5, 2 * BLK, DH), BF),
            pltpu.VMEM((5, 2 * BLK, DH), BF),
            pltpu.VMEM((5, DH, 2 * BLK), BF),
            pltpu.VMEM((5, DH + 16, 2 * BLK), BF),
            pltpu.VMEM((BLK, 2 * BLK), F32),
            pltpu.VMEM((pairs, 1, 2 * BLK), F32),
            pltpu.VMEM((4, pairs, 1, 2 * BLK), F32),
            pltpu.VMEM((pairs, DH + 16, 2 * BLK), F32),
            pltpu.VMEM((4, pairs, 2 * BLK, 2 * BLK), BF),
            pltpu.VMEM((4, pairs, 2 * BLK, 2 * BLK), F32),
            pltpu.VMEM((pairs, DH, 2 * BLK), F32),
            pltpu.VMEM((5, 2 * BLK, DH), F32),
            pltpu.VMEM((5, 2 * BLK, DH), F32),
            pltpu.VMEM(wide, BF),
            pltpu.VMEM(wide, BF),
            pltpu.VMEM((5, n_head, 2, 32, DH), BF),
            pltpu.VMEM((5, n_head, 2, 32, DH), BF),
            pltpu.VMEM((n_head, 2, 32, DH), BF),
            pltpu.VMEM((n_head, 2, 32, DH), BF),
            pltpu.VMEM((n_head, 2, 32, DH), BF),
            dma((4,)), dma((2,)),
            dma((7,)), dma((7,)), dma((4,)), dma((4,)),
            dma((4,)), dma((4,)), dma((7,)), dma((7,)),
        ],
        compiler_params=pltpu.CompilerParams(
            collective_id=0, has_side_effects=True, vmem_limit_bytes=56 * 2**20
        ),
        cost_estimate=pl.CostEstimate(flops=6500000000, bytes_accessed=5 * 2**20, transcendentals=4500000),
    )(lengths, query, keys, values, d_out)


def solution(mesh):
    in_specs = (
        P("ctx", "head"),
        P(("ctx", "head"), None),
        P(("ctx", "head"), None),
        P("ctx", "head"),
        P(),
    )
    out_specs = (
        P("ctx", "head"),
        P("ctx", "head"),
        P(("ctx", "head"), None),
        P(("ctx", "head"), None),
    )
    return jax.shard_map(local, mesh=mesh, in_specs=in_specs, out_specs=out_specs, check_vma=False)
```

```python
import functools
import math

import jax
import jax.numpy as jnp
from jax import lax
from jax.experimental import pallas as pl
from jax.experimental.pallas import tpu as pltpu
from jax.sharding import PartitionSpec as P

QH = 128
KVH = 8
DH = 128
BLK = 128
GROUP = QH // KVH
PAIRS = GROUP // 2
MESH = pl.DeviceIdType.MESH
BF = jnp.bfloat16
F32 = jnp.float32
SCALE = 1.0 / math.sqrt(DH)
C2 = SCALE * math.log2(math.e)
MASKED = -1e30


def dot(a, b):
    return lax.dot_general(a, b, (((1,), (0,)), ((), ())), preferred_element_type=F32)


def write_out(*refs):
    sem = refs[8]
    copies = [pltpu.make_async_copy(refs[n], refs[4 + n], sem.at[n]) for n in range(4)]
    for copy in copies:
        copy.start()
    for copy in copies:
        copy.wait()


def kernel(
    n_ctx, n_head,
    len_ref, q_hbm, k_hbm, v_hbm, do_hbm,
    o_out, dq_out, dk_ref, dv_ref,
    q_ref, do_ref, k_ref, v_ref, qt, dot_t, kv, kk, vv, kt, vte, tri,
    m_run, m_tile, acc, p_all, dp_all, dqt, dk_acc, dv_acc,
    gsend, grecv, gown, gfin, stage,
    load_sem, a_send, a_recv, c_send, c_recv, g_send, g_recv, b_send, b_recv,
):
    c = lax.axis_index("ctx")
    h = lax.axis_index("head")

    chips = n_head // 2
    order = [(0, 1)] + [(d, e) for d in (1, 3, 2) for e in (0, 1)]

    def head_at(d, e):
        return 2 * lax.rem(h // 2 + d, chips) + lax.rem(h + e, 2)

    def peer(j):
        return (c, head_at(*order[j - 1]))

    def after(o):
        return (lax.rem(c + o, n_ctx), h)

    def before(o):
        return (lax.rem(c + n_ctx - o, n_ctx), h)

    loads = [
        pltpu.make_async_copy(k_hbm, k_ref, load_sem.at[0]),
        pltpu.make_async_copy(v_hbm, v_ref, load_sem.at[1]),
        pltpu.make_async_copy(q_hbm, q_ref, load_sem.at[2]),
        pltpu.make_async_copy(do_hbm, do_ref, load_sem.at[3]),
    ]
    for copy in loads:
        copy.start()

    barrier = pltpu.get_barrier_semaphore()
    for j in range(1, n_head):
        pl.semaphore_signal(barrier, inc=1, device_id=peer(j), device_id_type=MESH)
    for o in range(1, 5):
        pl.semaphore_signal(barrier, inc=1, device_id=after(o), device_id_type=MESH)
        pl.semaphore_signal(barrier, inc=1, device_id=before(o), device_id_type=MESH)

    loads[0].wait()
    loads[1].wait()
    for j in range(n_head):
        stage[j, 0] = k_ref[:, j * DH:(j + 1) * DH]
        stage[j, 1] = v_ref[:, j * DH:(j + 1) * DH]
    kv[0, h] = stage[h]
    pl.semaphore_wait(barrier, n_head - 1 + 8)

    heads_in = {}
    for n, (d, e) in enumerate(order):
        target = head_at(d, e)
        copy = pltpu.make_async_remote_copy(
            src_ref=stage.at[target], dst_ref=kv.at[0, h],
            send_sem=a_send.at[n], recv_sem=a_recv.at[n],
            device_id=(c, target), device_id_type=MESH)
        copy.start()
        heads_in[d, e] = copy

    loads[2].wait()
    loads[3].wait()

    def transpose_pair(i, carry):
        u = i // PAIRS
        g = lax.rem(i, PAIRS)
        rows = pl.ds(pl.multiple_of(u * BLK, BLK), BLK)
        for e in range(2):
            cols = pl.ds(pl.multiple_of((2 * g + e) * DH, DH), DH)
            qt[i, :, e * BLK:(e + 1) * BLK] = q_ref[rows, cols].T
            dot_t[i, :, e * BLK:(e + 1) * BLK] = do_ref[rows, cols].T
        m_run[i] = jnp.full((1, 2 * BLK), 2 * MASKED, F32)
        acc[i] = jnp.zeros((DH + 16, 2 * BLK), F32)
        dqt[i] = jnp.zeros((DH, 2 * BLK), F32)
        return carry

    lax.fori_loop(0, 2 * PAIRS, transpose_pair, 0, unroll=2)
    key_at = lax.broadcasted_iota(jnp.int32, (BLK, 2 * BLK), 0)
    query_at = lax.rem(lax.broadcasted_iota(jnp.int32, (BLK, 2 * BLK), 1), BLK)
    tri[...] = jnp.where(key_at > query_at, MASKED, 0.0)
    dk_acc[...] = jnp.zeros_like(dk_acc)
    dv_acc[...] = jnp.zeros_like(dv_acc)

    starts = []
    for u in range(2):
        end = jnp.int32(0)
        first = jnp.int32(0)
        for d in range(16):
            end = end + len_ref[d]
            first = jnp.where(end <= 2 * c + u, end, first)
        starts.append(first)

    def onward(d, o):
        first = 2 * lax.rem(h // 2 + chips - d, chips)
        return first >= n_head // 2, pltpu.make_async_remote_copy(
            src_ref=kv.at[0, pl.ds(first, 2)], dst_ref=kv.at[o, pl.ds(first, 2)],
            send_sem=c_send.at[o - 1, d], recv_sem=c_recv.at[o - 1, d],
            device_id=after(o), device_id_type=MESH)

    def each_part(o, act):
        for d in range(chips):
            late, copy = onward(d, o)
            if o < 4:
                act(copy)
            else:
                pl.when(late)(functools.partial(act, copy))

    for d in (0, 1, 3, 2):
        for e in (0, 1):
            if (d, e) in heads_in:
                heads_in[d, e].wait_recv()
        for o in range(1, 5):
            late, copy = onward(d, o)
            if o < 4:
                copy.start()
            else:
                pl.when(late)(copy.start)

    def prepare(t):
        if t < 4:
            key = kv[t, :, 0].reshape(2 * BLK, DH)
            val = kv[t, :, 1].reshape(2 * BLK, DH)
        else:
            half = n_head // 2
            key = jnp.concatenate((kv[4, half:, 0].reshape(BLK, DH), kv[0, :half, 0].reshape(BLK, DH)), 0)
            val = jnp.concatenate((kv[4, half:, 1].reshape(BLK, DH), kv[0, :half, 1].reshape(BLK, DH)), 0)
        kk[t] = key
        vv[t] = val
        kt[t] = key.T
        vte[t, :DH] = val.T
        vte[t, DH:] = jnp.ones((16, 2 * BLK), BF)

    def place(u, t):
        return t if u == 1 else t - 1

    def forward(u, t):
        first_unit = 2 * c - 2 * t if t < 4 else 2 * c - 7
        bias0 = jnp.where(first_unit >= starts[u], 0.0, MASKED).astype(F32)
        bias1 = jnp.where(first_unit + 1 >= starts[u], 0.0, MASKED).astype(F32)
        slot = place(u, t)

        def one(g):
            i = u * PAIRS + g
            scores = dot(kk[t], qt[i])
            dp_all[slot, i] = dot(vv[t], dot_t[i])
            low = scores[:BLK] + bias0
            high = scores[BLK:] + (tri[...] if t in (0, 4) else bias1)
            old = m_run[i]
            new = jnp.maximum(old, jnp.max(jnp.maximum(low, high), axis=0, keepdims=True))
            p_low = jnp.exp2((low - new) * C2).astype(BF)
            p_high = jnp.exp2((high - new) * C2).astype(BF)
            weights = jnp.concatenate((p_low, p_high), 0)
            p_all[slot, i] = weights
            m_tile[slot, i] = new
            m_run[i] = new
            acc[i] = acc[i] * jnp.exp2((old - new) * C2) + dot(vte[t], weights)

        for g in range(PAIRS):
            one(g)

    prepare(0)
    forward(1, 0)
    for o in range(1, 4):
        each_part(o, lambda copy: copy.wait_recv())
        prepare(o)
        forward(0, o)
        forward(1, o)
    each_part(4, lambda copy: copy.wait_recv())
    prepare(4)
    forward(0, 4)

    for i in range(2 * PAIRS):
        inverse = 1.0 / acc[i, DH:DH + 1]
        low = (acc[i, :DH] * inverse).astype(BF)
        acc[i, DH:DH + 1] = inverse
        acc[i, DH + 8:DH + 9] = jnp.sum(low.astype(F32) * dot_t[i].astype(F32), axis=0, keepdims=True)

    def backward(u, t):
        slot = place(u, t)

        def one(g):
            i = u * PAIRS + g
            rows = pl.ds(u * BLK, BLK)
            first = pl.ds(2 * g * DH, DH)
            second = pl.ds((2 * g + 1) * DH, DH)
            queries = jnp.concatenate((q_ref[rows, first], q_ref[rows, second]), 0)
            cotangents = jnp.concatenate((do_ref[rows, first], do_ref[rows, second]), 0)
            factor = jnp.exp2((m_tile[slot, i] - m_run[i]) * C2) * acc[i, DH:DH + 1]
            weights = p_all[slot, i].astype(F32) * factor
            ds = (weights * (dp_all[slot, i] - acc[i, DH + 8:DH + 9])).astype(BF)
            dqt[i] += dot(kt[t], ds)
            return dot(ds, queries), dot(weights.astype(BF), cotangents)

        sums = [one(g) for g in range(PAIRS)]
        dk_acc[t] += sum(pair[0] for pair in sums)
        dv_acc[t] += sum(pair[1] for pair in sums)

    half = n_head // 2
    grads_out = []

    def send(o):
        if o < 4:
            gsend[o, :, 0] = (dk_acc[o] * SCALE).astype(BF).reshape(n_head, 32, DH)
            gsend[o, :, 1] = dv_acc[o].astype(BF).reshape(n_head, 32, DH)
            part, there = gsend.at[o], grecv.at[o]
        else:
            gsend[4, half:, 0] = (dk_acc[4, :BLK] * SCALE).astype(BF).reshape(half, 32, DH)
            gsend[4, half:, 1] = dv_acc[4, :BLK].astype(BF).reshape(half, 32, DH)
            part, there = gsend.at[4, pl.ds(half, half)], grecv.at[4, pl.ds(half, half)]
        copy = pltpu.make_async_remote_copy(
            src_ref=part, dst_ref=there,
            send_sem=g_send.at[o - 1], recv_sem=g_recv.at[o - 1],
            device_id=before(o), device_id_type=MESH)
        copy.start()
        grads_out.append(copy)

    backward(0, 4)
    send(4)
    for o in range(3, 0, -1):
        backward(0, o)
        backward(1, o)
        send(o)
    backward(1, 0)

    def finish(i, carry):
        u = i // PAIRS
        g = lax.rem(i, PAIRS)
        rows = pl.ds(pl.multiple_of(u * BLK, BLK), BLK)
        low = (dqt[i] * SCALE).astype(BF)
        out = (acc[i, :DH] * acc[i, DH:DH + 1]).astype(BF)
        for e in range(2):
            cols = pl.ds(pl.multiple_of((2 * g + e) * DH, DH), DH)
            dq_out[rows, cols] = low[:, e * BLK:(e + 1) * BLK].T
            o_out[rows, cols] = out[:, e * BLK:(e + 1) * BLK].T
        return carry

    lax.fori_loop(0, 2 * PAIRS, finish, 0, unroll=2)

    for copy in grads_out:
        copy.wait_recv()
    dk_low = dk_acc[0, :BLK] + dk_acc[4, BLK:]
    dv_low = dv_acc[0, :BLK] + dv_acc[4, BLK:]
    for n, (low, high, scale) in enumerate(
        ((dk_low, dk_acc[0, BLK:], SCALE), (dv_low, dv_acc[0, BLK:], 1.0))):
        low = (low * scale).reshape(half, 32, DH)
        high = (high * scale).reshape(half, 32, DH)
        for o in range(1, 4):
            low = low + grecv[o, :half, n].astype(F32)
            high = high + grecv[o, half:, n].astype(F32)
        high = high + grecv[4, half:, n].astype(F32)
        gown[:half, n] = low.astype(BF)
        gown[half:, n] = high.astype(BF)

    gfin[h] = gown[h]
    heads_out = []
    for n, (d, e) in enumerate(order):
        target = head_at(d, e)
        copy = pltpu.make_async_remote_copy(
            src_ref=gown.at[target], dst_ref=gfin.at[h],
            send_sem=b_send.at[n], recv_sem=b_recv.at[n],
            device_id=(c, target), device_id_type=MESH)
        copy.start()
        heads_out.append(copy)
    for copy in heads_in.values():
        copy.wait_send()
    for o in range(1, 5):
        each_part(o, lambda copy: copy.wait_send())
    for copy in grads_out:
        copy.wait_send()
    for copy in heads_out:
        copy.wait()
    for j in range(n_head):
        dk_ref[:, j * DH:(j + 1) * DH] = gfin[j, 0]
        dv_ref[:, j * DH:(j + 1) * DH] = gfin[j, 1]


def local(query, keys, values, d_out, lengths):
    n_ctx = lax.axis_size("ctx")
    n_head = lax.axis_size("head")
    pairs = 2 * PAIRS
    hbm = pl.BlockSpec(memory_space=pl.ANY)
    vmem = pl.BlockSpec(memory_space=pltpu.VMEM)
    wide = (2 * BLK, GROUP * DH)
    dma = pltpu.SemaphoreType.DMA
    held = pl.pallas_call(
        functools.partial(kernel, n_ctx, n_head),
        name="attention",
        out_shape=(
            pltpu.VMEM(query.shape, BF),
            pltpu.VMEM(query.shape, BF),
            pltpu.VMEM(keys.shape, BF),
            pltpu.VMEM(keys.shape, BF),
        ),
        in_specs=[pl.BlockSpec(memory_space=pltpu.SMEM), hbm, hbm, hbm, hbm],
        out_specs=(vmem, vmem, vmem, vmem),
        scratch_shapes=[
            pltpu.VMEM(wide, BF),
            pltpu.VMEM(wide, BF),
            pltpu.VMEM(keys.shape, BF),
            pltpu.VMEM(keys.shape, BF),
            pltpu.VMEM((pairs, DH, 2 * BLK), BF),
            pltpu.VMEM((pairs, DH, 2 * BLK), BF),
            pltpu.VMEM((5, n_head, 2, 32, DH), BF),
            pltpu.VMEM((5, 2 * BLK, DH), BF),
            pltpu.VMEM((5, 2 * BLK, DH), BF),
            pltpu.VMEM((5, DH, 2 * BLK), BF),
            pltpu.VMEM((5, DH + 16, 2 * BLK), BF),
            pltpu.VMEM((BLK, 2 * BLK), F32),
            pltpu.VMEM((pairs, 1, 2 * BLK), F32),
            pltpu.VMEM((4, pairs, 1, 2 * BLK), F32),
            pltpu.VMEM((pairs, DH + 16, 2 * BLK), F32),
            pltpu.VMEM((4, pairs, 2 * BLK, 2 * BLK), BF),
            pltpu.VMEM((4, pairs, 2 * BLK, 2 * BLK), F32),
            pltpu.VMEM((pairs, DH, 2 * BLK), F32),
            pltpu.VMEM((5, 2 * BLK, DH), F32),
            pltpu.VMEM((5, 2 * BLK, DH), F32),
            pltpu.VMEM((5, n_head, 2, 32, DH), BF),
            pltpu.VMEM((5, n_head, 2, 32, DH), BF),
            pltpu.VMEM((n_head, 2, 32, DH), BF),
            pltpu.VMEM((n_head, 2, 32, DH), BF),
            pltpu.VMEM((n_head, 2, 32, DH), BF),
            dma((4,)),
            dma((7,)), dma((7,)), dma((4, 4)), dma((4, 4)),
            dma((4,)), dma((4,)), dma((7,)), dma((7,)),
        ],
        compiler_params=pltpu.CompilerParams(
            collective_id=0, has_side_effects=True, vmem_limit_bytes=56 * 2**20
        ),
        cost_estimate=pl.CostEstimate(flops=6500000000, bytes_accessed=5 * 2**20, transcendentals=4500000),
    )(lengths, query, keys, values, d_out)
    return pl.pallas_call(
        write_out,
        name="write_out",
        out_shape=tuple(jax.ShapeDtypeStruct(x.shape, BF) for x in (query, query, keys, keys)),
        in_specs=[vmem] * 4,
        out_specs=(hbm,) * 4,
        scratch_shapes=[dma((4,))],
    )(*(pltpu.with_memory_space_constraint(x, pltpu.VMEM) for x in held))


def solution(mesh):
    in_specs = (
        P("ctx", "head"),
        P(("ctx", "head"), None),
        P(("ctx", "head"), None),
        P("ctx", "head"),
        P(),
    )
    out_specs = (
        P("ctx", "head"),
        P("ctx", "head"),
        P(("ctx", "head"), None),
        P(("ctx", "head"), None),
    )
    return jax.shard_map(local, mesh=mesh, in_specs=in_specs, out_specs=out_specs, check_vma=False)
```

```python
import functools
import math

import jax
import jax.numpy as jnp
from jax import lax
from jax.experimental import pallas as pl
from jax.experimental.pallas import tpu as pltpu
from jax.sharding import PartitionSpec as P

QH = 128
KVH = 8
DH = 128
BLK = 128
GROUP = QH // KVH
PAIRS = GROUP // 2
MESH = pl.DeviceIdType.MESH
BF = jnp.bfloat16
F32 = jnp.float32
SCALE = 1.0 / math.sqrt(DH)
C2 = SCALE * math.log2(math.e)
MASKED = -1e30


def dot(a, b):
    return lax.dot_general(a, b, (((1,), (0,)), ((), ())), preferred_element_type=F32)


def write_out(*refs):
    sem = refs[8]
    copies = [pltpu.make_async_copy(refs[n], refs[4 + n], sem.at[n]) for n in range(4)]
    for copy in copies:
        copy.start()
    for copy in copies:
        copy.wait()


def kernel(
    n_ctx, n_head,
    len_ref, q_hbm, k_hbm, v_hbm, do_hbm,
    o_out, dq_out, dk_ref, dv_ref,
    q_ref, do_ref, k_ref, v_ref, qt, dot_t, kv, kk, vv, kt, vte, tri,
    m_run, m_tile, acc, p_all, dp_all, s_all, dqt, dk_acc, dv_acc,
    gsend, grecv, own, gown, gfin, stage,
    load_sem, a_send, a_recv, c_send, c_recv, g_send, g_recv, b_send, b_recv,
):
    c = lax.axis_index("ctx")
    h = lax.axis_index("head")

    chips = n_head // 2
    order = [(0, 1)] + [(d, e) for d in (1, 3, 2) for e in (0, 1)]

    def head_at(d, e):
        return 2 * lax.rem(h // 2 + d, chips) + lax.rem(h + e, 2)

    def peer(j):
        return (c, head_at(*order[j - 1]))

    def after(o):
        return (lax.rem(c + o, n_ctx), h)

    def before(o):
        return (lax.rem(c + n_ctx - o, n_ctx), h)

    barrier = pltpu.get_barrier_semaphore()
    for j in range(1, n_head):
        pl.semaphore_signal(barrier, inc=1, device_id=peer(j), device_id_type=MESH)
    for o in range(1, 5):
        pl.semaphore_signal(barrier, inc=1, device_id=after(o), device_id_type=MESH)
        pl.semaphore_signal(barrier, inc=1, device_id=before(o), device_id_type=MESH)

    loads = [
        pltpu.make_async_copy(k_hbm, k_ref, load_sem.at[0]),
        pltpu.make_async_copy(v_hbm, v_ref, load_sem.at[1]),
        pltpu.make_async_copy(q_hbm, q_ref, load_sem.at[2]),
        pltpu.make_async_copy(do_hbm, do_ref, load_sem.at[3]),
    ]
    for copy in loads:
        copy.start()

    loads[0].wait()
    loads[1].wait()
    for j in range(n_head):
        stage[j, 0] = k_ref[:, j * DH:(j + 1) * DH]
        stage[j, 1] = v_ref[:, j * DH:(j + 1) * DH]
    kv[0, h] = stage[h]
    pl.semaphore_wait(barrier, n_head - 1 + 8)

    heads_in = {}
    for n, (d, e) in enumerate(order):
        target = head_at(d, e)
        copy = pltpu.make_async_remote_copy(
            src_ref=stage.at[target], dst_ref=kv.at[0, h],
            send_sem=a_send.at[n], recv_sem=a_recv.at[n],
            device_id=(c, target), device_id_type=MESH)
        copy.start()
        heads_in[d, e] = copy

    loads[2].wait()
    loads[3].wait()

    def transpose_pair(i, carry):
        u = i // PAIRS
        g = lax.rem(i, PAIRS)
        rows = pl.ds(pl.multiple_of(u * BLK, BLK), BLK)
        for e in range(2):
            cols = pl.ds(pl.multiple_of((2 * g + e) * DH, DH), DH)
            qt[i, :, e * BLK:(e + 1) * BLK] = q_ref[rows, cols].T
            dot_t[i, :, e * BLK:(e + 1) * BLK] = do_ref[rows, cols].T
        m_run[i] = jnp.full((1, 2 * BLK), 2 * MASKED, F32)
        acc[i] = jnp.zeros((DH + 16, 2 * BLK), F32)
        dqt[i] = jnp.zeros((DH, 2 * BLK), F32)
        return carry

    lax.fori_loop(0, 2 * PAIRS, transpose_pair, 0, unroll=2)
    key_at = lax.broadcasted_iota(jnp.int32, (BLK, 2 * BLK), 0)
    query_at = lax.rem(lax.broadcasted_iota(jnp.int32, (BLK, 2 * BLK), 1), BLK)
    tri[...] = jnp.where(key_at > query_at, MASKED, 0.0)
    dk_acc[...] = jnp.zeros_like(dk_acc)
    dv_acc[...] = jnp.zeros_like(dv_acc)

    starts = []
    for u in range(2):
        end = jnp.int32(0)
        first = jnp.int32(0)
        for d in range(16):
            end = end + len_ref[d]
            first = jnp.where(end <= 2 * c + u, end, first)
        starts.append(first)

    half = n_head // 2

    def onward(d, o):
        first = 2 * lax.rem(h // 2 + chips - d, chips)
        return first >= n_head // 2, pltpu.make_async_remote_copy(
            src_ref=kv.at[0, pl.ds(first, 2)], dst_ref=kv.at[o, pl.ds(first, 2)],
            send_sem=c_send.at[o - 1, d], recv_sem=c_recv.at[o - 1, d],
            device_id=after(o), device_id_type=MESH)

    def each_part(o, act):
        for d in range(chips):
            late, copy = onward(d, o)
            if o < 4:
                act(copy)
            else:
                pl.when(late)(functools.partial(act, copy))

    for d in (0, 1, 3, 2):
        for e in (0, 1):
            if (d, e) in heads_in:
                heads_in[d, e].wait_recv()
        for o in range(1, 5):
            late, copy = onward(d, o)
            if o < 4:
                copy.start()
            else:
                pl.when(late)(copy.start)

    def prepare(t):
        if t < 4:
            key = kv[t, :, 0].reshape(2 * BLK, DH)
            val = kv[t, :, 1].reshape(2 * BLK, DH)
        else:
            key = jnp.concatenate((kv[4, half:, 0].reshape(BLK, DH), kv[0, :half, 0].reshape(BLK, DH)), 0)
            val = jnp.concatenate((kv[4, half:, 1].reshape(BLK, DH), kv[0, :half, 1].reshape(BLK, DH)), 0)
        kk[t] = key
        vv[t] = val
        kt[t] = key.T
        vte[t, :DH] = val.T
        vte[t, DH:] = jnp.ones((16, 2 * BLK), BF)

    def place(u, t):
        return t if u == 1 else t - 1

    def forward(u, t):
        first_unit = 2 * c - 2 * t if t < 4 else 2 * c - 7
        bias0 = jnp.where(first_unit >= starts[u], 0.0, MASKED).astype(F32)
        bias1 = jnp.where(first_unit + 1 >= starts[u], 0.0, MASKED).astype(F32)
        slot = place(u, t)

        last = tri[...] if t in (0, 4) else bias1
        span = range(u * PAIRS, (u + 1) * PAIRS)
        for i in span:
            s_all[i % PAIRS] = dot(kk[t], qt[i])
            dp_all[slot, i] = dot(vv[t], dot_t[i])
        for i in span:
            g = i % PAIRS
            top = jnp.maximum(s_all[g, :BLK] + bias0, s_all[g, BLK:] + last)
            m_tile[slot, i] = jnp.maximum(m_run[i], jnp.max(top, axis=0, keepdims=True))
        for i in span:
            g = i % PAIRS
            new = m_tile[slot, i]
            p_all[slot, i, :BLK] = jnp.exp2((s_all[g, :BLK] + bias0 - new) * C2).astype(BF)
            p_all[slot, i, BLK:] = jnp.exp2((s_all[g, BLK:] + last - new) * C2).astype(BF)
            acc[i] = acc[i] * jnp.exp2((m_run[i] - new) * C2) + dot(vte[t], p_all[slot, i])
            m_run[i] = new

    prepare(0)
    forward(1, 0)
    for o in range(1, 4):
        each_part(o, lambda copy: copy.wait_recv())
        prepare(o)
        forward(1, o)
        forward(0, o)

    def close(u):
        for i in range(u * PAIRS, (u + 1) * PAIRS):
            inverse = 1.0 / acc[i, DH:DH + 1]
            low = (acc[i, :DH] * inverse).astype(BF)
            acc[i, DH:DH + 1] = inverse
            acc[i, DH + 8:DH + 9] = jnp.sum(low.astype(F32) * dot_t[i].astype(F32), axis=0, keepdims=True)

    def backward(u, t):
        slot = place(u, t)

        def one(g):
            i = u * PAIRS + g
            rows = pl.ds(u * BLK, BLK)
            first = pl.ds(2 * g * DH, DH)
            second = pl.ds((2 * g + 1) * DH, DH)
            queries = jnp.concatenate((q_ref[rows, first], q_ref[rows, second]), 0)
            cotangents = jnp.concatenate((do_ref[rows, first], do_ref[rows, second]), 0)
            factor = jnp.exp2((m_tile[slot, i] - m_run[i]) * C2) * acc[i, DH:DH + 1]
            weights = p_all[slot, i].astype(F32) * factor
            ds = (weights * (dp_all[slot, i] - acc[i, DH + 8:DH + 9])).astype(BF)
            dqt[i] += dot(kt[t], ds)
            return dot(ds, queries), dot(weights.astype(BF), cotangents)

        sums = [one(g) for g in range(PAIRS)]
        dk_acc[t] += sum(pair[0] for pair in sums)
        dv_acc[t] += sum(pair[1] for pair in sums)

    out_order = (2, 1, 3, 0)

    def back(d, o):
        first = 2 * lax.rem(h // 2 + d, chips)
        return first, pltpu.make_async_remote_copy(
            src_ref=gsend.at[o, pl.ds(first, 2)], dst_ref=grecv.at[o, pl.ds(first, 2)],
            send_sem=g_send.at[o - 1, d], recv_sem=g_recv.at[o - 1, d],
            device_id=before(o), device_id_type=MESH)

    def each_back(d, o, act):
        first, copy = back(d, o)
        if o < 4:
            act(copy)
        else:
            pl.when(first >= half)(functools.partial(act, copy))

    def send(o):
        if o < 4:
            gsend[o, :, 0] = (dk_acc[o] * SCALE).astype(BF).reshape(n_head, 32, DH)
            gsend[o, :, 1] = dv_acc[o].astype(BF).reshape(n_head, 32, DH)
        else:
            gsend[4, half:, 0] = (dk_acc[4, :BLK] * SCALE).astype(BF).reshape(half, 32, DH)
            gsend[4, half:, 1] = dv_acc[4, :BLK].astype(BF).reshape(half, 32, DH)
        for d in out_order:
            each_back(d, o, lambda copy: copy.start())

    grecv[4, :half] = jnp.zeros((half, 2, 32, DH), BF)
    close(1)
    each_part(4, lambda copy: copy.wait_recv())
    prepare(4)
    forward(0, 4)
    close(0)
    backward(0, 4)
    send(4)
    backward(0, 3)
    backward(1, 3)
    send(3)
    backward(0, 2)
    backward(1, 2)
    send(2)
    backward(0, 1)
    backward(1, 1)
    send(1)
    backward(1, 0)

    own[:, 0] = (dk_acc[0] * SCALE).reshape(n_head, 32, DH)
    own[:, 1] = dv_acc[0].reshape(n_head, 32, DH)
    own[:half, 0] += (dk_acc[4, BLK:] * SCALE).reshape(half, 32, DH)
    own[:half, 1] += dv_acc[4, BLK:].reshape(half, 32, DH)

    def finish(i, carry):
        u = i // PAIRS
        g = lax.rem(i, PAIRS)
        rows = pl.ds(pl.multiple_of(u * BLK, BLK), BLK)
        low = (dqt[i] * SCALE).astype(BF)
        out = (acc[i, :DH] * acc[i, DH:DH + 1]).astype(BF)
        for e in range(2):
            cols = pl.ds(pl.multiple_of((2 * g + e) * DH, DH), DH)
            dq_out[rows, cols] = low[:, e * BLK:(e + 1) * BLK].T
            o_out[rows, cols] = out[:, e * BLK:(e + 1) * BLK].T
        return carry

    lax.fori_loop(0, 2 * PAIRS, finish, 0, unroll=2)

    heads_out = []
    for d in out_order:
        for o in range(4, 0, -1):
            each_back(d, o, lambda copy: copy.wait_recv())
        first = 2 * lax.rem(h // 2 + d, chips)
        part = pl.ds(first, 2)
        total = own[part]
        for o in range(1, 5):
            total = total + grecv[o, part].astype(F32)
        gown[part] = total.astype(BF)
        for e in (0, 1):
            if (d, e) == (0, 0):
                continue
            n = order.index((d, e))
            target = head_at(d, e)
            copy = pltpu.make_async_remote_copy(
                src_ref=gown.at[target], dst_ref=gfin.at[h],
                send_sem=b_send.at[n], recv_sem=b_recv.at[n],
                device_id=(c, target), device_id_type=MESH)
            copy.start()
            heads_out.append(copy)
    gfin[h] = gown[h]
    for copy in heads_in.values():
        copy.wait_send()
    for o in range(1, 5):
        each_part(o, lambda copy: copy.wait_send())
    for d in out_order:
        for o in range(1, 5):
            each_back(d, o, lambda copy: copy.wait_send())
    for copy in heads_out:
        copy.wait()
    for j in range(n_head):
        dk_ref[:, j * DH:(j + 1) * DH] = gfin[j, 0]
        dv_ref[:, j * DH:(j + 1) * DH] = gfin[j, 1]


def local(query, keys, values, d_out, lengths):
    n_ctx = lax.axis_size("ctx")
    n_head = lax.axis_size("head")
    pairs = 2 * PAIRS
    hbm = pl.BlockSpec(memory_space=pl.ANY)
    vmem = pl.BlockSpec(memory_space=pltpu.VMEM)
    wide = (2 * BLK, GROUP * DH)
    dma = pltpu.SemaphoreType.DMA
    held = pl.pallas_call(
        functools.partial(kernel, n_ctx, n_head),
        name="attention",
        out_shape=(
            pltpu.VMEM(query.shape, BF),
            pltpu.VMEM(query.shape, BF),
            pltpu.VMEM(keys.shape, BF),
            pltpu.VMEM(keys.shape, BF),
        ),
        in_specs=[pl.BlockSpec(memory_space=pltpu.SMEM), hbm, hbm, hbm, hbm],
        out_specs=(vmem, vmem, vmem, vmem),
        scratch_shapes=[
            pltpu.VMEM(wide, BF),
            pltpu.VMEM(wide, BF),
            pltpu.VMEM(keys.shape, BF),
            pltpu.VMEM(keys.shape, BF),
            pltpu.VMEM((pairs, DH, 2 * BLK), BF),
            pltpu.VMEM((pairs, DH, 2 * BLK), BF),
            pltpu.VMEM((5, n_head, 2, 32, DH), BF),
            pltpu.VMEM((5, 2 * BLK, DH), BF),
            pltpu.VMEM((5, 2 * BLK, DH), BF),
            pltpu.VMEM((5, DH, 2 * BLK), BF),
            pltpu.VMEM((5, DH + 16, 2 * BLK), BF),
            pltpu.VMEM((BLK, 2 * BLK), F32),
            pltpu.VMEM((pairs, 1, 2 * BLK), F32),
            pltpu.VMEM((4, pairs, 1, 2 * BLK), F32),
            pltpu.VMEM((pairs, DH + 16, 2 * BLK), F32),
            pltpu.VMEM((4, pairs, 2 * BLK, 2 * BLK), BF),
            pltpu.VMEM((4, pairs, 2 * BLK, 2 * BLK), F32),
            pltpu.VMEM((PAIRS, 2 * BLK, 2 * BLK), F32),
            pltpu.VMEM((pairs, DH, 2 * BLK), F32),
            pltpu.VMEM((5, 2 * BLK, DH), F32),
            pltpu.VMEM((5, 2 * BLK, DH), F32),
            pltpu.VMEM((5, n_head, 2, 32, DH), BF),
            pltpu.VMEM((5, n_head, 2, 32, DH), BF),
            pltpu.VMEM((n_head, 2, 32, DH), F32),
            pltpu.VMEM((n_head, 2, 32, DH), BF),
            pltpu.VMEM((n_head, 2, 32, DH), BF),
            pltpu.VMEM((n_head, 2, 32, DH), BF),
            dma((4,)),
            dma((7,)), dma((7,)), dma((4, 4)), dma((4, 4)),
            dma((4, 4)), dma((4, 4)), dma((7,)), dma((7,)),
        ],
        compiler_params=pltpu.CompilerParams(
            collective_id=0, has_side_effects=True, vmem_limit_bytes=56 * 2**20
        ),
        cost_estimate=pl.CostEstimate(flops=6500000000, bytes_accessed=5 * 2**20, transcendentals=4500000),
    )(lengths, query, keys, values, d_out)
    return pl.pallas_call(
        write_out,
        name="write_out",
        out_shape=tuple(jax.ShapeDtypeStruct(x.shape, BF) for x in (query, query, keys, keys)),
        in_specs=[vmem] * 4,
        out_specs=(hbm,) * 4,
        scratch_shapes=[dma((4,))],
    )(*(pltpu.with_memory_space_constraint(x, pltpu.VMEM) for x in held))


def solution(mesh):
    in_specs = (
        P("ctx", "head"),
        P(("ctx", "head"), None),
        P(("ctx", "head"), None),
        P("ctx", "head"),
        P(),
    )
    out_specs = (
        P("ctx", "head"),
        P("ctx", "head"),
        P(("ctx", "head"), None),
        P(("ctx", "head"), None),
    )
    return jax.shard_map(local, mesh=mesh, in_specs=in_specs, out_specs=out_specs, check_vma=False)
```

```python
import functools
import math

import jax
import jax.numpy as jnp
from jax import lax
from jax.experimental import pallas as pl
from jax.experimental.pallas import tpu as pltpu
from jax.sharding import PartitionSpec as P

QH = 128
KVH = 8
DH = 128
BLK = 128
GROUP = QH // KVH
PAIRS = GROUP // 2
MESH = pl.DeviceIdType.MESH
BF = jnp.bfloat16
F32 = jnp.float32
SCALE = 1.0 / math.sqrt(DH)
C2 = SCALE * math.log2(math.e)
MASKED = -1e30


def dot(a, b):
    return lax.dot_general(a, b, (((1,), (0,)), ((), ())), preferred_element_type=F32)


def write_out(*refs):
    sem = refs[8]
    copies = [pltpu.make_async_copy(refs[n], refs[4 + n], sem.at[n]) for n in (2, 3)]
    for n in range(2):
        for part in range(4):
            rows = pl.ds(part * 64, 64)
            copies.append(pltpu.make_async_copy(
                refs[n].at[rows], refs[4 + n].at[rows], sem.at[4 + 4 * n + part]))
    for copy in copies:
        copy.start()
    for copy in copies:
        copy.wait()


def kernel(
    n_ctx, n_head,
    len_ref, q_hbm, k_hbm, v_hbm, do_hbm,
    o_out, dq_out, dk_ref, dv_ref,
    q_ref, do_ref, k_ref, v_ref, qt, dot_t, kv, kk, vv, kt, vte, tri,
    m_run, m_tile, acc, p_all, dp_all, s_all, dqt, dk_acc, dv_acc,
    gsend, grecv, own, gown, gfin, stage,
    load_sem, a_send, a_recv, c_send, c_recv, g_send, g_recv, b_send, b_recv,
):
    c = lax.axis_index("ctx")
    h = lax.axis_index("head")

    chips = n_head // 2
    order = [(0, 1)] + [(d, e) for d in (1, 3, 2) for e in (0, 1)]

    def head_at(d, e):
        return 2 * lax.rem(h // 2 + d, chips) + lax.rem(h + e, 2)

    def peer(j):
        return (c, head_at(*order[j - 1]))

    def after(o):
        return (lax.rem(c + o, n_ctx), h)

    def before(o):
        return (lax.rem(c + n_ctx - o, n_ctx), h)

    barrier = pltpu.get_barrier_semaphore()
    for j in range(1, n_head):
        pl.semaphore_signal(barrier, inc=1, device_id=peer(j), device_id_type=MESH)
    for o in range(1, 5):
        pl.semaphore_signal(barrier, inc=1, device_id=after(o), device_id_type=MESH)
        pl.semaphore_signal(barrier, inc=1, device_id=before(o), device_id_type=MESH)

    loads = [
        pltpu.make_async_copy(k_hbm, k_ref, load_sem.at[0]),
        pltpu.make_async_copy(v_hbm, v_ref, load_sem.at[1]),
        pltpu.make_async_copy(q_hbm, q_ref, load_sem.at[2]),
        pltpu.make_async_copy(do_hbm, do_ref, load_sem.at[3]),
    ]
    for copy in loads:
        copy.start()

    loads[0].wait()
    loads[1].wait()
    for j in range(n_head):
        stage[j, 0] = k_ref[:, j * DH:(j + 1) * DH]
        stage[j, 1] = v_ref[:, j * DH:(j + 1) * DH]
    kv[0, h] = stage[h]
    pl.semaphore_wait(barrier, n_head - 1 + 8)

    heads_in = {}
    for n, (d, e) in enumerate(order):
        target = head_at(d, e)
        copy = pltpu.make_async_remote_copy(
            src_ref=stage.at[target], dst_ref=kv.at[0, h],
            send_sem=a_send.at[n], recv_sem=a_recv.at[n],
            device_id=(c, target), device_id_type=MESH)
        copy.start()
        heads_in[d, e] = copy

    def onward(d, o):
        first = 2 * lax.rem(h // 2 + chips - d, chips)
        return first >= n_head // 2, pltpu.make_async_remote_copy(
            src_ref=kv.at[0, pl.ds(first, 2)], dst_ref=kv.at[o, pl.ds(first, 2)],
            send_sem=c_send.at[o - 1, d], recv_sem=c_recv.at[o - 1, d],
            device_id=after(o), device_id_type=MESH)

    def each_part(o, act):
        for d in range(chips):
            late, copy = onward(d, o)
            if o < 4:
                act(copy)
            else:
                pl.when(late)(functools.partial(act, copy))

    def push(d, places):
        for e in (0, 1):
            if (d, e) in heads_in and (d, e) not in arrived:
                heads_in[d, e].wait_recv()
                arrived.add((d, e))
        for o in places:
            last, copy = onward(d, o)
            if o < 4:
                copy.start()
            else:
                pl.when(last)(copy.start)

    def transpose_pair(i, carry):
        u = i // PAIRS
        g = lax.rem(i, PAIRS)
        rows = pl.ds(pl.multiple_of(u * BLK, BLK), BLK)
        for e in range(2):
            cols = pl.ds(pl.multiple_of((2 * g + e) * DH, DH), DH)
            qt[i, :, e * BLK:(e + 1) * BLK] = q_ref[rows, cols].T
            dot_t[i, :, e * BLK:(e + 1) * BLK] = do_ref[rows, cols].T
        m_run[i] = jnp.full((1, 2 * BLK), 2 * MASKED, F32)
        acc[i] = jnp.zeros((DH + 16, 2 * BLK), F32)
        dqt[i] = jnp.zeros((DH, 2 * BLK), F32)
        return carry

    arrived = set()
    push(0, (1, 2))
    loads[2].wait()
    loads[3].wait()
    lax.fori_loop(PAIRS, 2 * PAIRS, transpose_pair, 0, unroll=2)
    push(1, (1, 2))
    push(3, (1, 2))
    lax.fori_loop(0, PAIRS, transpose_pair, 0, unroll=2)
    push(2, (1, 2))
    for o in [3, 4]:
        for d in (0, 1, 3, 2):
            push(d, (o,))
    key_at = lax.broadcasted_iota(jnp.int32, (BLK, 2 * BLK), 0)
    query_at = lax.rem(lax.broadcasted_iota(jnp.int32, (BLK, 2 * BLK), 1), BLK)
    tri[...] = jnp.where(key_at > query_at, MASKED, 0.0)
    dk_acc[...] = jnp.zeros_like(dk_acc)
    dv_acc[...] = jnp.zeros_like(dv_acc)

    starts = []
    for u in range(2):
        end = jnp.int32(0)
        first = jnp.int32(0)
        for d in range(16):
            end = end + len_ref[d]
            first = jnp.where(end <= 2 * c + u, end, first)
        starts.append(first)

    half = n_head // 2

    def prepare(t):
        if t < 4:
            key = kv[t, :, 0].reshape(2 * BLK, DH)
            val = kv[t, :, 1].reshape(2 * BLK, DH)
        else:
            key = jnp.concatenate((kv[4, half:, 0].reshape(BLK, DH), kv[0, :half, 0].reshape(BLK, DH)), 0)
            val = jnp.concatenate((kv[4, half:, 1].reshape(BLK, DH), kv[0, :half, 1].reshape(BLK, DH)), 0)
        kk[t] = key
        vv[t] = val
        kt[t] = key.T
        vte[t, :DH] = val.T
        vte[t, DH:] = jnp.ones((16, 2 * BLK), BF)

    def place(u, t):
        return t if u == 1 else t - 1

    def forward(u, t):
        first_unit = 2 * c - 2 * t if t < 4 else 2 * c - 7
        bias0 = jnp.where(first_unit >= starts[u], 0.0, MASKED).astype(F32)
        bias1 = jnp.where(first_unit + 1 >= starts[u], 0.0, MASKED).astype(F32)
        slot = place(u, t)

        last = tri[...] if t in (0, 4) else bias1
        span = range(u * PAIRS, (u + 1) * PAIRS)
        for i in span:
            s_all[i % PAIRS] = dot(kk[t], qt[i])
            dp_all[slot, i] = dot(vv[t], dot_t[i])
        for i in span:
            g = i % PAIRS
            top = jnp.maximum(s_all[g, :BLK] + bias0, s_all[g, BLK:] + last)
            m_tile[slot, i] = jnp.maximum(m_run[i], jnp.max(top, axis=0, keepdims=True))
        for i in span:
            g = i % PAIRS
            new = m_tile[slot, i]
            p_all[slot, i, :BLK] = jnp.exp2((s_all[g, :BLK] + bias0 - new) * C2).astype(BF)
            p_all[slot, i, BLK:] = jnp.exp2((s_all[g, BLK:] + last - new) * C2).astype(BF)
            acc[i] = acc[i] * jnp.exp2((m_run[i] - new) * C2) + dot(vte[t], p_all[slot, i])
            m_run[i] = new

    prepare(0)
    forward(1, 0)
    for o in range(1, 4):
        each_part(o, lambda copy: copy.wait_recv())
        prepare(o)
        forward(1, o)
        forward(0, o)

    def close(u):
        for i in range(u * PAIRS, (u + 1) * PAIRS):
            inverse = 1.0 / acc[i, DH:DH + 1]
            low = (acc[i, :DH] * inverse).astype(BF)
            acc[i, DH:DH + 1] = inverse
            acc[i, DH + 8:DH + 9] = jnp.sum(low.astype(F32) * dot_t[i].astype(F32), axis=0, keepdims=True)

    def backward(u, t):
        slot = place(u, t)

        def one(g):
            i = u * PAIRS + g
            rows = pl.ds(u * BLK, BLK)
            first = pl.ds(2 * g * DH, DH)
            second = pl.ds((2 * g + 1) * DH, DH)
            queries = jnp.concatenate((q_ref[rows, first], q_ref[rows, second]), 0)
            cotangents = jnp.concatenate((do_ref[rows, first], do_ref[rows, second]), 0)
            factor = jnp.exp2((m_tile[slot, i] - m_run[i]) * C2) * acc[i, DH:DH + 1]
            weights = p_all[slot, i].astype(F32) * factor
            ds = (weights * (dp_all[slot, i] - acc[i, DH + 8:DH + 9])).astype(BF)
            dqt[i] += dot(kt[t], ds)
            return dot(ds, queries), dot(weights.astype(BF), cotangents)

        sums = [one(g) for g in range(PAIRS)]
        dk_acc[t] += sum(pair[0] for pair in sums)
        dv_acc[t] += sum(pair[1] for pair in sums)

    out_order = (2, 1, 3, 0)

    def back(o):
        part = pl.ds(0, n_head) if o < 4 else pl.ds(half, half)
        return pltpu.make_async_remote_copy(
            src_ref=gsend.at[o, part], dst_ref=grecv.at[o, part],
            send_sem=g_send.at[o - 1], recv_sem=g_recv.at[o - 1],
            device_id=before(o), device_id_type=MESH)

    def send(o):
        if o < 4:
            gsend[o, :, 0] = (dk_acc[o] * SCALE).astype(BF).reshape(n_head, 32, DH)
            gsend[o, :, 1] = dv_acc[o].astype(BF).reshape(n_head, 32, DH)
        else:
            gsend[4, half:, 0] = (dk_acc[4, :BLK] * SCALE).astype(BF).reshape(half, 32, DH)
            gsend[4, half:, 1] = dv_acc[4, :BLK].astype(BF).reshape(half, 32, DH)
        back(o).start()

    grecv[4, :half] = jnp.zeros((half, 2, 32, DH), BF)
    close(1)
    each_part(4, lambda copy: copy.wait_recv())
    prepare(4)
    forward(0, 4)
    close(0)
    backward(0, 4)
    send(4)
    backward(0, 3)
    backward(1, 3)
    send(3)
    backward(0, 2)
    backward(1, 2)
    send(2)
    backward(0, 1)
    backward(1, 1)
    send(1)
    backward(1, 0)

    own[:, 0] = (dk_acc[0] * SCALE).reshape(n_head, 32, DH)
    own[:, 1] = dv_acc[0].reshape(n_head, 32, DH)
    own[:half, 0] += (dk_acc[4, BLK:] * SCALE).reshape(half, 32, DH)
    own[:half, 1] += dv_acc[4, BLK:].reshape(half, 32, DH)

    def finish(i, carry):
        u = i // PAIRS
        g = lax.rem(i, PAIRS)
        rows = pl.ds(pl.multiple_of(u * BLK, BLK), BLK)
        low = (dqt[i] * SCALE).astype(BF)
        out = (acc[i, :DH] * acc[i, DH:DH + 1]).astype(BF)
        for e in range(2):
            cols = pl.ds(pl.multiple_of((2 * g + e) * DH, DH), DH)
            dq_out[rows, cols] = low[:, e * BLK:(e + 1) * BLK].T
            o_out[rows, cols] = out[:, e * BLK:(e + 1) * BLK].T
        return carry

    lax.fori_loop(0, 2 * PAIRS, finish, 0, unroll=2)

    heads_out = []
    for o in range(4, 0, -1):
        back(o).wait_recv()
    for d in out_order:
        first = 2 * lax.rem(h // 2 + d, chips)
        part = pl.ds(first, 2)
        total = own[part]
        for o in range(1, 5):
            total = total + grecv[o, part].astype(F32)
        gown[part] = total.astype(BF)
        for e in (0, 1):
            if (d, e) == (0, 0):
                continue
            n = order.index((d, e))
            target = head_at(d, e)
            copy = pltpu.make_async_remote_copy(
                src_ref=gown.at[target], dst_ref=gfin.at[h],
                send_sem=b_send.at[n], recv_sem=b_recv.at[n],
                device_id=(c, target), device_id_type=MESH)
            copy.start()
            heads_out.append(copy)
    gfin[h] = gown[h]
    for copy in heads_in.values():
        copy.wait_send()
    for o in range(1, 5):
        each_part(o, lambda copy: copy.wait_send())
    for o in range(1, 5):
        back(o).wait_send()
    for copy in heads_out:
        copy.wait()
    for j in range(n_head):
        dk_ref[:, j * DH:(j + 1) * DH] = gfin[j, 0]
        dv_ref[:, j * DH:(j + 1) * DH] = gfin[j, 1]


def local(query, keys, values, d_out, lengths):
    n_ctx = lax.axis_size("ctx")
    n_head = lax.axis_size("head")
    pairs = 2 * PAIRS
    hbm = pl.BlockSpec(memory_space=pl.ANY)
    vmem = pl.BlockSpec(memory_space=pltpu.VMEM)
    wide = (2 * BLK, GROUP * DH)
    dma = pltpu.SemaphoreType.DMA
    held = pl.pallas_call(
        functools.partial(kernel, n_ctx, n_head),
        name="attention",
        out_shape=(
            pltpu.VMEM(query.shape, BF),
            pltpu.VMEM(query.shape, BF),
            pltpu.VMEM(keys.shape, BF),
            pltpu.VMEM(keys.shape, BF),
        ),
        in_specs=[pl.BlockSpec(memory_space=pltpu.SMEM), hbm, hbm, hbm, hbm],
        out_specs=(vmem, vmem, vmem, vmem),
        scratch_shapes=[
            pltpu.VMEM(wide, BF),
            pltpu.VMEM(wide, BF),
            pltpu.VMEM(keys.shape, BF),
            pltpu.VMEM(keys.shape, BF),
            pltpu.VMEM((pairs, DH, 2 * BLK), BF),
            pltpu.VMEM((pairs, DH, 2 * BLK), BF),
            pltpu.VMEM((5, n_head, 2, 32, DH), BF),
            pltpu.VMEM((5, 2 * BLK, DH), BF),
            pltpu.VMEM((5, 2 * BLK, DH), BF),
            pltpu.VMEM((5, DH, 2 * BLK), BF),
            pltpu.VMEM((5, DH + 16, 2 * BLK), BF),
            pltpu.VMEM((BLK, 2 * BLK), F32),
            pltpu.VMEM((pairs, 1, 2 * BLK), F32),
            pltpu.VMEM((4, pairs, 1, 2 * BLK), F32),
            pltpu.VMEM((pairs, DH + 16, 2 * BLK), F32),
            pltpu.VMEM((4, pairs, 2 * BLK, 2 * BLK), BF),
            pltpu.VMEM((4, pairs, 2 * BLK, 2 * BLK), F32),
            pltpu.VMEM((PAIRS, 2 * BLK, 2 * BLK), F32),
            pltpu.VMEM((pairs, DH, 2 * BLK), F32),
            pltpu.VMEM((5, 2 * BLK, DH), F32),
            pltpu.VMEM((5, 2 * BLK, DH), F32),
            pltpu.VMEM((5, n_head, 2, 32, DH), BF),
            pltpu.VMEM((5, n_head, 2, 32, DH), BF),
            pltpu.VMEM((n_head, 2, 32, DH), F32),
            pltpu.VMEM((n_head, 2, 32, DH), BF),
            pltpu.VMEM((n_head, 2, 32, DH), BF),
            pltpu.VMEM((n_head, 2, 32, DH), BF),
            dma((4,)),
            dma((7,)), dma((7,)), dma((4, 4)), dma((4, 4)),
            dma((4,)), dma((4,)), dma((7,)), dma((7,)),
        ],
        compiler_params=pltpu.CompilerParams(
            collective_id=0, has_side_effects=True, vmem_limit_bytes=56 * 2**20
        ),
        cost_estimate=pl.CostEstimate(flops=6500000000, bytes_accessed=5 * 2**20, transcendentals=4500000),
    )(lengths, query, keys, values, d_out)
    return pl.pallas_call(
        write_out,
        name="write_out",
        out_shape=tuple(jax.ShapeDtypeStruct(x.shape, BF) for x in (query, query, keys, keys)),
        in_specs=[vmem] * 4,
        out_specs=(hbm,) * 4,
        scratch_shapes=[dma((12,))],
    )(*(pltpu.with_memory_space_constraint(x, pltpu.VMEM) for x in held))


def solution(mesh):
    in_specs = (
        P("ctx", "head"),
        P(("ctx", "head"), None),
        P(("ctx", "head"), None),
        P("ctx", "head"),
        P(),
    )
    out_specs = (
        P("ctx", "head"),
        P("ctx", "head"),
        P(("ctx", "head"), None),
        P(("ctx", "head"), None),
    )
    return jax.shard_map(local, mesh=mesh, in_specs=in_specs, out_specs=out_specs, check_vma=False)
```

```python
import functools
import math

import jax
import jax.numpy as jnp
from jax import lax
from jax.experimental import pallas as pl
from jax.experimental.pallas import tpu as pltpu
from jax.sharding import PartitionSpec as P

QH = 128
KVH = 8
DH = 128
BLK = 128
GROUP = QH // KVH
PAIRS = GROUP // 2
MESH = pl.DeviceIdType.MESH
BF = jnp.bfloat16
F32 = jnp.float32
SCALE = 1.0 / math.sqrt(DH)
C2 = SCALE * math.log2(math.e)
MASKED = -1e30


def dot(a, b):
    return lax.dot_general(a, b, (((1,), (0,)), ((), ())), preferred_element_type=F32)


def write_out(*refs):
    sem = refs[8]
    copies = [pltpu.make_async_copy(refs[n], refs[4 + n], sem.at[n]) for n in (2, 3)]
    for n in range(2):
        for part in range(4):
            rows = pl.ds(part * 64, 64)
            copies.append(pltpu.make_async_copy(
                refs[n].at[rows], refs[4 + n].at[rows], sem.at[4 + 4 * n + part]))
    for copy in copies:
        copy.start()
    for copy in copies:
        copy.wait()


def kernel(
    n_ctx, n_head,
    len_ref, q_hbm, k_hbm, v_hbm, do_hbm,
    o_out, dq_out, dk_ref, dv_ref,
    q_ref, do_ref, k_ref, v_ref, qt, dot_t, kv, kk, vv, kt, vte, tri,
    m_run, m_tile, acc, p_all, dp_all, s_all, dqt, dk_acc, dv_acc,
    gsend, grecv, own, gown, gfin, stage,
    load_sem, a_send, a_recv, c_send, c_recv, g_send, g_recv, b_send, b_recv,
):
    c = lax.axis_index("ctx")
    h = lax.axis_index("head")

    chips = n_head // 2
    order = [(0, 1)] + [(d, e) for d in (2, 1, 3) for e in (0, 1)]

    def head_at(d, e):
        return 2 * lax.rem(h // 2 + d, chips) + lax.rem(h + e, 2)

    def peer(j):
        return (c, head_at(*order[j - 1]))

    def after(o):
        return (lax.rem(c + o, n_ctx), h)

    def before(o):
        return (lax.rem(c + n_ctx - o, n_ctx), h)

    barrier = pltpu.get_barrier_semaphore()
    for j in range(1, n_head):
        pl.semaphore_signal(barrier, inc=1, device_id=peer(j), device_id_type=MESH)
    for o in range(1, 5):
        pl.semaphore_signal(barrier, inc=1, device_id=after(o), device_id_type=MESH)
        pl.semaphore_signal(barrier, inc=1, device_id=before(o), device_id_type=MESH)

    loads = [
        pltpu.make_async_copy(k_hbm, k_ref, load_sem.at[0]),
        pltpu.make_async_copy(v_hbm, v_ref, load_sem.at[1]),
        pltpu.make_async_copy(q_hbm, q_ref, load_sem.at[2]),
        pltpu.make_async_copy(do_hbm, do_ref, load_sem.at[3]),
    ]
    for copy in loads:
        copy.start()

    loads[0].wait()
    loads[1].wait()
    for j in range(n_head):
        stage[j, 0] = k_ref[:, j * DH:(j + 1) * DH]
        stage[j, 1] = v_ref[:, j * DH:(j + 1) * DH]
    kv[0, h] = stage[h]
    pl.semaphore_wait(barrier, n_head - 1 + 8)

    heads_in = {}
    for n, (d, e) in enumerate(order):
        target = head_at(d, e)
        copy = pltpu.make_async_remote_copy(
            src_ref=stage.at[target], dst_ref=kv.at[0, h],
            send_sem=a_send.at[n], recv_sem=a_recv.at[n],
            device_id=(c, target), device_id_type=MESH)
        copy.start()
        heads_in[d, e] = copy

    def onward(d, o):
        first = 2 * lax.rem(h // 2 + chips - d, chips)
        return first >= n_head // 2, pltpu.make_async_remote_copy(
            src_ref=kv.at[0, pl.ds(first, 2)], dst_ref=kv.at[o, pl.ds(first, 2)],
            send_sem=c_send.at[o - 1, d], recv_sem=c_recv.at[o - 1, d],
            device_id=after(o), device_id_type=MESH)

    def each_part(o, act):
        for d in range(chips):
            late, copy = onward(d, o)
            if o < 4:
                act(copy)
            else:
                pl.when(late)(functools.partial(act, copy))

    def push(d, places):
        for e in (0, 1):
            if (d, e) in heads_in and (d, e) not in arrived:
                heads_in[d, e].wait_recv()
                arrived.add((d, e))
        for o in places:
            last, copy = onward(d, o)
            if o < 4:
                copy.start()
            else:
                pl.when(last)(copy.start)

    def transpose_pair(i, carry):
        u = i // PAIRS
        g = lax.rem(i, PAIRS)
        rows = pl.ds(pl.multiple_of(u * BLK, BLK), BLK)
        for e in range(2):
            cols = pl.ds(pl.multiple_of((2 * g + e) * DH, DH), DH)
            qt[i, :, e * BLK:(e + 1) * BLK] = q_ref[rows, cols].T
            dot_t[i, :, e * BLK:(e + 1) * BLK] = do_ref[rows, cols].T
        m_run[i] = jnp.full((1, 2 * BLK), 2 * MASKED, F32)
        acc[i] = jnp.zeros((DH + 16, 2 * BLK), F32)
        dqt[i] = jnp.zeros((DH, 2 * BLK), F32)
        return carry

    arrived = set()
    push(0, (1, 2))
    loads[2].wait()
    loads[3].wait()
    lax.fori_loop(PAIRS, 2 * PAIRS, transpose_pair, 0, unroll=2)
    push(1, (1, 2))
    push(3, (1, 2))
    lax.fori_loop(0, PAIRS, transpose_pair, 0, unroll=2)
    push(2, (1, 2))
    for o in [3, 4]:
        for d in (0, 1, 3, 2):
            push(d, (o,))
    key_at = lax.broadcasted_iota(jnp.int32, (BLK, 2 * BLK), 0)
    query_at = lax.rem(lax.broadcasted_iota(jnp.int32, (BLK, 2 * BLK), 1), BLK)
    tri[...] = jnp.where(key_at > query_at, MASKED, 0.0)
    dk_acc[...] = jnp.zeros_like(dk_acc)
    dv_acc[...] = jnp.zeros_like(dv_acc)

    starts = []
    for u in range(2):
        end = jnp.int32(0)
        first = jnp.int32(0)
        for d in range(16):
            end = end + len_ref[d]
            first = jnp.where(end <= 2 * c + u, end, first)
        starts.append(first)

    half = n_head // 2

    def prepare(t):
        if t < 4:
            key = kv[t, :, 0].reshape(2 * BLK, DH)
            val = kv[t, :, 1].reshape(2 * BLK, DH)
        else:
            key = jnp.concatenate((kv[4, half:, 0].reshape(BLK, DH), kv[0, :half, 0].reshape(BLK, DH)), 0)
            val = jnp.concatenate((kv[4, half:, 1].reshape(BLK, DH), kv[0, :half, 1].reshape(BLK, DH)), 0)
        kk[t] = key
        vv[t] = val
        kt[t] = key.T
        vte[t, :DH] = val.T
        vte[t, DH:] = jnp.ones((16, 2 * BLK), BF)

    def place(u, t):
        return t if u == 1 else t - 1

    def forward(u, t):
        first_unit = 2 * c - 2 * t if t < 4 else 2 * c - 7
        bias0 = jnp.where(first_unit >= starts[u], 0.0, MASKED).astype(F32)
        bias1 = jnp.where(first_unit + 1 >= starts[u], 0.0, MASKED).astype(F32)
        slot = place(u, t)

        last = tri[...] if t in (0, 4) else bias1
        span = range(u * PAIRS, (u + 1) * PAIRS)
        for i in span:
            s_all[i % PAIRS] = dot(kk[t], qt[i])
            dp_all[slot, i] = dot(vv[t], dot_t[i])
        for i in span:
            g = i % PAIRS
            top = jnp.maximum(s_all[g, :BLK] + bias0, s_all[g, BLK:] + last)
            m_tile[slot, i] = jnp.maximum(m_run[i], jnp.max(top, axis=0, keepdims=True))
        for i in span:
            g = i % PAIRS
            new = m_tile[slot, i]
            p_all[slot, i, :BLK] = jnp.exp2((s_all[g, :BLK] + bias0 - new) * C2).astype(BF)
            p_all[slot, i, BLK:] = jnp.exp2((s_all[g, BLK:] + last - new) * C2).astype(BF)
            acc[i] = acc[i] * jnp.exp2((m_run[i] - new) * C2) + dot(vte[t], p_all[slot, i])
            m_run[i] = new

    prepare(0)
    forward(1, 0)
    for o in range(1, 4):
        each_part(o, lambda copy: copy.wait_recv())
        prepare(o)
        forward(1, o)
        forward(0, o)

    def close(u):
        for i in range(u * PAIRS, (u + 1) * PAIRS):
            inverse = 1.0 / acc[i, DH:DH + 1]
            low = (acc[i, :DH] * inverse).astype(BF)
            acc[i, DH:DH + 1] = inverse
            acc[i, DH + 8:DH + 9] = jnp.sum(low.astype(F32) * dot_t[i].astype(F32), axis=0, keepdims=True)

    def backward(u, t):
        slot = place(u, t)

        def one(g):
            i = u * PAIRS + g
            rows = pl.ds(u * BLK, BLK)
            first = pl.ds(2 * g * DH, DH)
            second = pl.ds((2 * g + 1) * DH, DH)
            queries = jnp.concatenate((q_ref[rows, first], q_ref[rows, second]), 0)
            cotangents = jnp.concatenate((do_ref[rows, first], do_ref[rows, second]), 0)
            factor = jnp.exp2((m_tile[slot, i] - m_run[i]) * C2) * acc[i, DH:DH + 1]
            weights = p_all[slot, i].astype(F32) * factor
            ds = (weights * (dp_all[slot, i] - acc[i, DH + 8:DH + 9])).astype(BF)
            dqt[i] += dot(kt[t], ds)
            return dot(ds, queries), dot(weights.astype(BF), cotangents)

        sums = [one(g) for g in range(PAIRS)]
        dk_acc[t] += sum(pair[0] for pair in sums)
        dv_acc[t] += sum(pair[1] for pair in sums)

    out_order = (2, 1, 3, 0)

    def back(o):
        part = pl.ds(0, n_head) if o < 4 else pl.ds(half, half)
        return pltpu.make_async_remote_copy(
            src_ref=gsend.at[o, part], dst_ref=grecv.at[o, part],
            send_sem=g_send.at[o - 1], recv_sem=g_recv.at[o - 1],
            device_id=before(o), device_id_type=MESH)

    def send(o):
        if o < 4:
            gsend[o, :, 0] = (dk_acc[o] * SCALE).astype(BF).reshape(n_head, 32, DH)
            gsend[o, :, 1] = dv_acc[o].astype(BF).reshape(n_head, 32, DH)
        else:
            gsend[4, half:, 0] = (dk_acc[4, :BLK] * SCALE).astype(BF).reshape(half, 32, DH)
            gsend[4, half:, 1] = dv_acc[4, :BLK].astype(BF).reshape(half, 32, DH)
        back(o).start()

    grecv[4, :half] = jnp.zeros((half, 2, 32, DH), BF)
    close(1)
    each_part(4, lambda copy: copy.wait_recv())
    prepare(4)
    forward(0, 4)
    close(0)
    backward(0, 4)
    send(4)
    backward(0, 3)
    backward(1, 3)
    send(3)
    backward(0, 2)
    backward(1, 2)
    send(2)
    backward(0, 1)
    backward(1, 1)
    send(1)
    backward(1, 0)

    own[:, 0] = (dk_acc[0] * SCALE).reshape(n_head, 32, DH)
    own[:, 1] = dv_acc[0].reshape(n_head, 32, DH)
    own[:half, 0] += (dk_acc[4, BLK:] * SCALE).reshape(half, 32, DH)
    own[:half, 1] += dv_acc[4, BLK:].reshape(half, 32, DH)

    def finish(i, carry):
        u = i // PAIRS
        g = lax.rem(i, PAIRS)
        rows = pl.ds(pl.multiple_of(u * BLK, BLK), BLK)
        low = (dqt[i] * SCALE).astype(BF)
        out = (acc[i, :DH] * acc[i, DH:DH + 1]).astype(BF)
        for e in range(2):
            cols = pl.ds(pl.multiple_of((2 * g + e) * DH, DH), DH)
            dq_out[rows, cols] = low[:, e * BLK:(e + 1) * BLK].T
            o_out[rows, cols] = out[:, e * BLK:(e + 1) * BLK].T
        return carry

    lax.fori_loop(0, 2 * PAIRS, finish, 0, unroll=2)

    heads_out = []
    for o in range(4, 0, -1):
        back(o).wait_recv()
    for d in out_order:
        first = 2 * lax.rem(h // 2 + d, chips)
        part = pl.ds(first, 2)
        total = own[part]
        for o in range(1, 5):
            total = total + grecv[o, part].astype(F32)
        gown[part] = total.astype(BF)
        for e in (0, 1):
            if (d, e) == (0, 0):
                continue
            n = order.index((d, e))
            target = head_at(d, e)
            copy = pltpu.make_async_remote_copy(
                src_ref=gown.at[target], dst_ref=gfin.at[h],
                send_sem=b_send.at[n], recv_sem=b_recv.at[n],
                device_id=(c, target), device_id_type=MESH)
            copy.start()
            heads_out.append(copy)
    gfin[h] = gown[h]
    for copy in heads_in.values():
        copy.wait_send()
    for o in range(1, 5):
        each_part(o, lambda copy: copy.wait_send())
    for o in range(1, 5):
        back(o).wait_send()
    for copy in heads_out:
        copy.wait()
    for j in range(n_head):
        dk_ref[:, j * DH:(j + 1) * DH] = gfin[j, 0]
        dv_ref[:, j * DH:(j + 1) * DH] = gfin[j, 1]


def local(query, keys, values, d_out, lengths):
    n_ctx = lax.axis_size("ctx")
    n_head = lax.axis_size("head")
    pairs = 2 * PAIRS
    hbm = pl.BlockSpec(memory_space=pl.ANY)
    vmem = pl.BlockSpec(memory_space=pltpu.VMEM)
    wide = (2 * BLK, GROUP * DH)
    dma = pltpu.SemaphoreType.DMA
    held = pl.pallas_call(
        functools.partial(kernel, n_ctx, n_head),
        name="attention",
        out_shape=(
            pltpu.VMEM(query.shape, BF),
            pltpu.VMEM(query.shape, BF),
            pltpu.VMEM(keys.shape, BF),
            pltpu.VMEM(keys.shape, BF),
        ),
        in_specs=[pl.BlockSpec(memory_space=pltpu.SMEM), hbm, hbm, hbm, hbm],
        out_specs=(vmem, vmem, vmem, vmem),
        scratch_shapes=[
            pltpu.VMEM(wide, BF),
            pltpu.VMEM(wide, BF),
            pltpu.VMEM(keys.shape, BF),
            pltpu.VMEM(keys.shape, BF),
            pltpu.VMEM((pairs, DH, 2 * BLK), BF),
            pltpu.VMEM((pairs, DH, 2 * BLK), BF),
            pltpu.VMEM((5, n_head, 2, 32, DH), BF),
            pltpu.VMEM((5, 2 * BLK, DH), BF),
            pltpu.VMEM((5, 2 * BLK, DH), BF),
            pltpu.VMEM((5, DH, 2 * BLK), BF),
            pltpu.VMEM((5, DH + 16, 2 * BLK), BF),
            pltpu.VMEM((BLK, 2 * BLK), F32),
            pltpu.VMEM((pairs, 1, 2 * BLK), F32),
            pltpu.VMEM((4, pairs, 1, 2 * BLK), F32),
            pltpu.VMEM((pairs, DH + 16, 2 * BLK), F32),
            pltpu.VMEM((4, pairs, 2 * BLK, 2 * BLK), BF),
            pltpu.VMEM((4, pairs, 2 * BLK, 2 * BLK), F32),
            pltpu.VMEM((PAIRS, 2 * BLK, 2 * BLK), F32),
            pltpu.VMEM((pairs, DH, 2 * BLK), F32),
            pltpu.VMEM((5, 2 * BLK, DH), F32),
            pltpu.VMEM((5, 2 * BLK, DH), F32),
            pltpu.VMEM((5, n_head, 2, 32, DH), BF),
            pltpu.VMEM((5, n_head, 2, 32, DH), BF),
            pltpu.VMEM((n_head, 2, 32, DH), F32),
            pltpu.VMEM((n_head, 2, 32, DH), BF),
            pltpu.VMEM((n_head, 2, 32, DH), BF),
            pltpu.VMEM((n_head, 2, 32, DH), BF),
            dma((4,)),
            dma((7,)), dma((7,)), dma((4, 4)), dma((4, 4)),
            dma((4,)), dma((4,)), dma((7,)), dma((7,)),
        ],
        compiler_params=pltpu.CompilerParams(
            collective_id=0, has_side_effects=True, vmem_limit_bytes=56 * 2**20
        ),
        cost_estimate=pl.CostEstimate(flops=6500000000, bytes_accessed=5 * 2**20, transcendentals=4500000),
    )(lengths, query, keys, values, d_out)
    return pl.pallas_call(
        write_out,
        name="write_out",
        out_shape=tuple(jax.ShapeDtypeStruct(x.shape, BF) for x in (query, query, keys, keys)),
        in_specs=[vmem] * 4,
        out_specs=(hbm,) * 4,
        scratch_shapes=[dma((12,))],
    )(*(pltpu.with_memory_space_constraint(x, pltpu.VMEM) for x in held))


def solution(mesh):
    in_specs = (
        P("ctx", "head"),
        P(("ctx", "head"), None),
        P(("ctx", "head"), None),
        P("ctx", "head"),
        P(),
    )
    out_specs = (
        P("ctx", "head"),
        P("ctx", "head"),
        P(("ctx", "head"), None),
        P(("ctx", "head"), None),
    )
    return jax.shard_map(local, mesh=mesh, in_specs=in_specs, out_specs=out_specs, check_vma=False)
```
